32 devices in a mesh: section: 2 (over core), fsdp: 4 (over y, x), replica: 4 (over z).
Axes of the slice: x: 2, y: 2, z: 4, core: 2. Of those that a mesh axis runs over, the one named last changes fastest.
Arguments:
- inputs: bfloat16 [24576, 576], P(('fsdp', 'replica')), may hold values from -6 to 6
- cotangent: bfloat16 [24576, 576], P(('fsdp', 'replica')), may hold values from -6 to 6
- seq_lengths: int32 [32, 4], P(('fsdp', 'replica')), may hold values from 1 to 640, 768 in all within a row
- attn_gain: bfloat16 [2, 576], P('section', 'fsdp'), may hold values from 0.5 to 1.5
- w_query: bfloat16 [2, 576, 576], P('section', 'fsdp'), may hold values from -0.25 to 0.25
- key_value_weight: bfloat16 [2, 576, 384], P('section', 'fsdp'), may hold values from -0.25 to 0.25
- w_out: bfloat16 [2, 576, 576], P('section', 'fsdp'), may hold values from -1.5 to 1.5
- ffn_gain: bfloat16 [2, 576], P('section', 'fsdp'), may hold values from 0.5 to 1.5
- w_gateup: bfloat16 [2, 576, 3072], P('section', 'fsdp'), may hold values from -0.25 to 0.25
- w_down: bfloat16 [2, 1536, 576], P('section', 'fsdp'), may hold values from -0.15625 to 0.15625
Outputs:
- activations: bfloat16 [2, 24576, 576], P('section', ('fsdp', 'replica'))
- input_grads: float32 [2, 24576, 576], P('section', ('fsdp', 'replica'))
- grad_attn_gain: float32 [2, 576], P('section', 'fsdp')
- grad_query: float32 [2, 576, 576], P('section', 'fsdp')
- grad_keyval: float32 [2, 576, 384], P('section', 'fsdp')
- grad_out: float32 [2, 576, 576], P('section', 'fsdp')
- grad_ffn_gain: float32 [2, 576], P('section', 'fsdp')
- grad_gateup: float32 [2, 576, 3072], P('section', 'fsdp')
- grad_down: float32 [2, 1536, 576], P('section', 'fsdp')
The draws below stay inside these ranges and needn't reach their ends.
Inputs may be any that keep to these rules, and one draw needn't show every extreme that they name: `seq_lengths`: each row holds the lengths of the 4 sequences of one micro-batch in order; a row sums to 768 and its largest entry is exactly 640.
All inputs are finite; a program needn't handle non-finite values.
Results may differ from the reference program's by a relative error of at most 0.023.
Values may be sent and summed in bfloat16 or wider, within the bound.
A program may use at most 256 MiB of HBM per device.

```python
import math
import jax
import jax.numpy as jnp
import numpy as np
from jax import lax

MODEL_WIDTH = 576
QUERY_HEADS = 9
KEY_VALUE_HEADS = 3
HEAD_SIZE = 64
FF = 1536
MB_TOK = 768
SEQS = 4
LONGEST = 640
SLOTS = 32
TOKENS = 24576


def block_scale(stream_key, shape, split, low, high):
    gain = 1.0
    for axis_at, parts in split:
        draws = jax.random.uniform(jax.random.fold_in(jax.random.fold_in(stream_key, 6), axis_at), (parts,), jnp.float32, low / len(split), high / len(split))
        gain = gain * jnp.repeat(jnp.exp(draws), shape[axis_at] // parts).reshape((-1,) + (1,) * (len(shape) - 1 - axis_at))
    return gain


def length_profile(number_of, total, bound, slope):
    weights = [(1 << 20) // math.isqrt(rank ** slope) + 1 for rank in range(2, number_of + 1)]
    surplus, holding = total - bound - (number_of - 1), [1] * (number_of - 1)
    while surplus > 0:
        candidates = [i for i in range(number_of - 1) if holding[i] < bound]
        whole, remaining = sum([weights[i] for i in candidates]), surplus
        for i in candidates:
            extra = min(bound - holding[i], max(1, remaining * weights[i] // whole), surplus)
            holding[i] = holding[i] + extra
            surplus = surplus - extra
    return np.array([bound] + holding)


def uneven_parts(stream_key, number_of, total, bound, slope):
    if number_of == 2:
        one = jax.random.randint(stream_key, (), max(1, total - bound), min(bound, total - 1) + 1)
        return jnp.stack([one, total - one])
    sizes = jnp.asarray(length_profile(number_of, total, bound, slope), jnp.int32)
    twos = (number_of - 1) // 2
    giver, sink = sizes[1:1 + 2 * twos:2], sizes[2:2 + 2 * twos:2]
    slack = jnp.minimum(giver - 1, bound - sink)
    passed = jax.random.randint(jax.random.fold_in(stream_key, 1), (twos,), 0, 1 << 20) % (slack + 1)
    sizes = sizes.at[1:1 + 2 * twos:2].set(giver - passed).at[2:2 + 2 * twos:2].set(sink + passed)
    return sizes[jax.random.permutation(jax.random.fold_in(stream_key, 2), number_of)]


def normal_values(rng, dims, spread, most, cuts=(), held_as=jnp.bfloat16):
    level = block_scale(rng, dims, cuts, -0.22, 0.18) if cuts else 1.0
    result = jax.random.normal(rng, dims, jnp.float32) * spread * level
    return jnp.minimum(jnp.maximum(result, -most), most).astype(held_as)


def setup_inputs(seed: int = 0) -> dict:
    seeds = jax.random.split(jax.random.key(seed), 11)
    inputs = normal_values(seeds[0], (TOKENS, MODEL_WIDTH), 1.0, 6.0, ((0, 16),))
    cotangent = normal_values(seeds[1], (TOKENS, MODEL_WIDTH), 1.0, 6.0, ((0, 16),))
    seq_lengths = jax.vmap(lambda own: uneven_parts(own, SEQS, MB_TOK, LONGEST, 2))(jax.random.split(seeds[2], SLOTS)).reshape((SLOTS, SEQS)).astype(jnp.int32)
    attn_gain = jnp.clip(1.0 + 0.1 * jax.random.normal(seeds[3], (2, MODEL_WIDTH), jnp.float32), 0.5, 1.5).astype(jnp.bfloat16)
    w_query = normal_values(seeds[4], (2, MODEL_WIDTH, QUERY_HEADS * HEAD_SIZE), MODEL_WIDTH ** -0.5, 0.25, ((0, 2), (1, 4)))
    key_value_weight = normal_values(seeds[5], (2, MODEL_WIDTH, 2 * KEY_VALUE_HEADS * HEAD_SIZE), MODEL_WIDTH ** -0.5, 0.25, ((0, 2), (1, 4)))
    w_out = normal_values(seeds[6], (2, QUERY_HEADS * HEAD_SIZE, MODEL_WIDTH), 16 ** -0.5, 1.5, ((0, 2), (1, 4)))
    ffn_gain = jnp.clip(1.0 + 0.1 * jax.random.normal(seeds[7], (2, MODEL_WIDTH), jnp.float32), 0.5, 1.5).astype(jnp.bfloat16)
    w_gateup = normal_values(seeds[8], (2, MODEL_WIDTH, 2 * FF), MODEL_WIDTH ** -0.5, 0.25, ((0, 2), (1, 4)))
    w_down = normal_values(seeds[9], (2, FF, MODEL_WIDTH), FF ** -0.5, 0.15625, ((0, 2), (1, 4)))
    return dict(inputs=inputs, cotangent=cotangent, seq_lengths=seq_lengths, attn_gain=attn_gain, w_query=w_query, key_value_weight=key_value_weight, w_out=w_out, ffn_gain=ffn_gain, w_gateup=w_gateup, w_down=w_down)


@jax.custom_vjp
def low(v):
    return lax.optimization_barrier(v.astype(jnp.bfloat16)).astype(jnp.float32)

@jax.custom_vjp
def low_back(v):
    return v

def low_keep(v):
    return (low(v), None)

def low_pass(kept, grad):
    return (grad,)

def back_keep(v):
    return (v, None)

def back_low(kept, grad):
    return (low(grad),)
low.defvjp(low_keep, low_pass)
low_back.defvjp(back_keep, back_low)
EPS = 1e-05
ROPE_BASE = 100000.0

def positions(lengths, token_count):
    ends = jnp.cumsum(lengths)
    index = jnp.arange(token_count, dtype=jnp.int32)
    after = index[:, None] >= ends[None, :]
    segment = lax.optimization_barrier(jnp.sum(after.astype(jnp.int32), 1))
    place = index - lax.optimization_barrier(jnp.sum(jnp.where(after, lengths[None, :], 0), 1))
    return (segment, place)

def rope_tables(place, width):
    half = width // 2
    freq = ROPE_BASE ** (-(jnp.arange(half, dtype=jnp.float32) * 2.0 / width))
    angle = place.astype(jnp.float32)[:, None] * freq[None, :]
    angle = jnp.concatenate([angle, angle], 1)
    return (jnp.cos(angle)[:, None, :], jnp.sin(angle)[:, None, :])

def rotary_apply(value_rows, cosine_table, sine_table):
    half = value_rows.shape[-1] // 2
    turned = jnp.concatenate([-value_rows[..., half:], value_rows[..., :half]], -1)
    return value_rows * cosine_table + turned * sine_table

def layer(hidden_in, gain_one, w_q, w_kv, w_o, gain_two, w_gu, w_d, segment, place):
    highest = lax.Precision.HIGHEST
    token_count = hidden_in.shape[0]
    query_group_size = QUERY_HEADS // KEY_VALUE_HEADS
    cosine_table, sine_table = rope_tables(place, HEAD_SIZE)
    scale_in = lax.rsqrt(lax.optimization_barrier(jnp.mean(hidden_in * hidden_in, -1, keepdims=True)) + EPS)
    normed = low(hidden_in * scale_in * gain_one)
    query_single = low_back(jnp.dot(normed, w_q, precision=highest))
    key_value_rows = low_back(jnp.dot(normed, w_kv, precision=highest))
    query_rows = low(rotary_apply(query_single.reshape(token_count, QUERY_HEADS, HEAD_SIZE), cosine_table, sine_table)).reshape(token_count, KEY_VALUE_HEADS, query_group_size, HEAD_SIZE)
    key_rows = low(rotary_apply(key_value_rows[:, :KEY_VALUE_HEADS * HEAD_SIZE].reshape(token_count, KEY_VALUE_HEADS, HEAD_SIZE), cosine_table, sine_table))
    value_rows = low(key_value_rows[:, KEY_VALUE_HEADS * HEAD_SIZE:].reshape(token_count, KEY_VALUE_HEADS, HEAD_SIZE))
    index = jnp.arange(token_count, dtype=jnp.int32)
    allowed = (segment[:, None] == segment[None, :]) & (index[None, :] <= index[:, None])
    scores = low_back(jnp.einsum('qkgd,tkd->kgqt', query_rows, key_rows, precision=highest) * HEAD_SIZE ** (-0.5))
    scores = jnp.where(allowed, scores, -1e+30)
    peak = lax.optimization_barrier(jnp.max(scores, -1, keepdims=True))
    expo = jnp.exp(scores - peak)
    prob = low(expo / lax.optimization_barrier(jnp.sum(expo, -1, keepdims=True)))
    attended = jnp.einsum('kgqt,tkd->qkgd', prob, value_rows, precision=highest).reshape(token_count, QUERY_HEADS * HEAD_SIZE)
    attended = low_back(low(attended))
    mixed = hidden_in + low_back(jnp.dot(attended, w_o, precision=highest))
    scale_mid = lax.rsqrt(lax.optimization_barrier(jnp.mean(mixed * mixed, -1, keepdims=True)) + EPS)
    normed_two = low(mixed * scale_mid * gain_two)
    gateup = low_back(jnp.dot(normed_two, w_gu, precision=highest))
    inner = low(jax.nn.silu(gateup[:, :FF]) * gateup[:, FF:])
    return mixed + low_back(jnp.dot(inner, w_d, precision=highest))

def reference(inputs, cotangent, seq_lengths, attn_gain, w_query, key_value_weight, w_out, ffn_gain, w_gateup, w_down):
    stacks = (attn_gain, w_query, key_value_weight, w_out, ffn_gain, w_gateup, w_down)
    first_weights = tuple((w[0].astype(jnp.float32) for w in stacks))
    second_weights = tuple((w[1].astype(jnp.float32) for w in stacks))
    x_slots = inputs.astype(jnp.float32).reshape(SLOTS, MB_TOK, MODEL_WIDTH)
    cot_slots = cotangent.astype(jnp.float32).reshape(SLOTS, MB_TOK, MODEL_WIDTH)

    def one_slot(carry, packed):
        x_slot, cot_slot, lengths = packed
        segment, place = positions(lengths, MB_TOK)

        def apply(hidden_in, *weights):
            return layer(hidden_in, *weights, segment, place)
        first_out, first_back = jax.vjp(apply, x_slot, *first_weights)
        middle = low(first_out)
        second_out, second_back = jax.vjp(apply, middle, *second_weights)
        grads_two = second_back(cot_slot)
        grads_one = first_back(low(grads_two[0]))
        carry_one = tuple((c + g for c, g in zip(carry[0], grads_one[1:])))
        carry_two = tuple((c + g for c, g in zip(carry[1], grads_two[1:])))
        return ((carry_one, carry_two), (first_out.astype(jnp.bfloat16), second_out.astype(jnp.bfloat16), grads_one[0], grads_two[0]))
    zero_filled = tuple((jnp.zeros_like(w) for w in first_weights))
    totals, results = lax.scan(one_slot, (zero_filled, zero_filled), (x_slots, cot_slots, seq_lengths))
    act_one, act_two, grad_one, grad_two = results
    activations = jnp.stack([act_one.reshape(TOKENS, MODEL_WIDTH), act_two.reshape(TOKENS, MODEL_WIDTH)])
    input_grads = jnp.stack([grad_one.reshape(TOKENS, MODEL_WIDTH), grad_two.reshape(TOKENS, MODEL_WIDTH)])
    grads = [jnp.stack([totals[0][j], totals[1][j]]) for j in range(7)]
    return (activations, input_grads, grads[0], grads[1], grads[2], grads[3], grads[4], grads[5], grads[6])
```

```python
import functools

import jax
import jax.numpy as jnp
from jax import lax
from jax.experimental import pallas as pl
from jax.experimental.pallas import tpu as pltpu
from jax.sharding import PartitionSpec as P

QUERY_HEADS = 9
KEY_VALUE_HEADS = 3
GROUP = 3
HEAD_SIZE = 64
FF = 1536
MICRO = 2
EPS = 1e-05
ROPE_BASE = 100000.0
Q_BLOCK = 256
LIMIT = 56 * 1024 * 1024
BF = jnp.bfloat16
F32 = jnp.float32


def positions(lengths, token_count):
    ends = jnp.cumsum(lengths)
    index = jnp.arange(token_count, dtype=jnp.int32)
    after = index[:, None] >= ends[None, :]
    start = jnp.sum(jnp.where(after, lengths[None, :], 0), 1)
    return start, index - start


def rope_tables(place):
    half = HEAD_SIZE // 2
    freq = ROPE_BASE ** (-(jnp.arange(half, dtype=F32) * 2.0 / HEAD_SIZE))
    angle = place.astype(F32)[:, None] * freq[None, :]
    cosine, sine = jnp.cos(angle), jnp.sin(angle)
    return (
        jnp.concatenate([cosine] * 4, 1),
        jnp.concatenate([-sine, sine, -sine, sine], 1),
    )


def turned(x):
    lane = lax.broadcasted_iota(jnp.int32, x.shape, 1)
    first = (lane % HEAD_SIZE) < HEAD_SIZE // 2
    return jnp.where(first, pltpu.roll(x, 96, 1), pltpu.roll(x, 32, 1))


def fill_bias(bias, start_ref):
    tokens = bias.shape[0]
    start = start_ref[...]
    for first in range(0, tokens, 128):
        key = lax.broadcasted_iota(jnp.int32, (128, tokens), 0) + first
        query = lax.broadcasted_iota(jnp.int32, (128, tokens), 1)
        ok = (key >= start) & (key <= query)
        bias[first : first + 128, :] = jnp.where(ok, 0.0, -1e30)


def dot_t(a, b):
    return lax.dot_general(a, b, (((1,), (1,)), ((), ())), preferred_element_type=F32)


def dot_0(a, b):
    return lax.dot_general(a, b, (((0,), (0,)), ((), ())), preferred_element_type=F32)


def attention_forward(qkv_ref, cos_ref, sin_ref, start_ref, att_ref, q_ref, k_ref, v_ref, lse_ref, bias, o_s):
    tokens = qkv_ref.shape[0]
    fill_bias(bias, start_ref)
    cosine, sine = cos_ref[...], sin_ref[...]
    for chunk in range(6):
        x = qkv_ref[:, chunk * 128 : chunk * 128 + 128]
        x = x * cosine + turned(x) * sine
        for side in range(2):
            head = chunk * 2 + side
            part = x[:, side * 64 : side * 64 + 64]
            if head < QUERY_HEADS:
                q_ref[head] = (part * HEAD_SIZE ** (-0.5)).astype(BF)
            else:
                k_ref[head - QUERY_HEADS] = part.astype(BF)
    for head in range(KEY_VALUE_HEADS):
        v_ref[head] = qkv_ref[:, 768 + head * 64 : 832 + head * 64].astype(BF)

    def group(g, _):
        for first in range(0, tokens, Q_BLOCK):
            limit = first + Q_BLOCK
            queries = q_ref[pl.ds(g * GROUP, GROUP), first:limit, :].reshape(GROUP * Q_BLOCK, HEAD_SIZE)
            scores = dot_t(k_ref[g, :limit, :], queries)
            mask = bias[:limit, first:limit]
            probs = []
            for head in range(GROUP):
                s = scores[:, head * Q_BLOCK : (head + 1) * Q_BLOCK] + mask
                peak = jnp.max(s, 0, keepdims=True)
                e = jnp.exp(s - peak)
                total = jnp.sum(e, 0, keepdims=True)
                lse_ref[g * GROUP + head, :, first:limit] = peak + jnp.log(total)
                probs.append((e * (1.0 / total)).astype(BF))
            prob = jnp.concatenate(probs, 1)
            out = dot_0(prob, v_ref[g, :limit, :])
            o_s[pl.ds(g * GROUP, GROUP), first:limit, :] = out.reshape(GROUP, Q_BLOCK, HEAD_SIZE)
        return 0

    lax.fori_loop(0, KEY_VALUE_HEADS, group, 0)
    for head in range(0, QUERY_HEADS - 1, 2):
        att_ref[:, head * 64 : head * 64 + 128] = jnp.concatenate([o_s[head], o_s[head + 1]], 1).astype(BF)
    att_ref[:, 512:576] = o_s[8].astype(BF)


def attention_backward(
    q_ref, k_ref, v_ref, lse_ref, att_ref, datt_ref, cos_ref, sin_ref, start_ref, out_ref,
    bias, do_s, delta_s, dqk_s, dv_s,
):
    tokens = att_ref.shape[0]
    fill_bias(bias, start_ref)
    ones = jnp.ones((8, HEAD_SIZE), BF)
    for head in range(QUERY_HEADS):
        cols = slice(head * 64, head * 64 + 64)
        grad = datt_ref[:, cols]
        do_s[head] = grad
        product = (grad.astype(F32) * att_ref[:, cols].astype(F32)).astype(BF)
        delta_s[head] = dot_t(ones, product)
    dqk_s[QUERY_HEADS:] = jnp.zeros((KEY_VALUE_HEADS, tokens, HEAD_SIZE), F32)
    dv_s[...] = jnp.zeros_like(dv_s)

    def group(g, _):
        for first in range(0, tokens, Q_BLOCK):
            limit = first + Q_BLOCK
            heads = pl.ds(g * GROUP, GROUP)
            queries = q_ref[heads, first:limit, :].reshape(GROUP * Q_BLOCK, HEAD_SIZE)
            grads = do_s[heads, first:limit, :].reshape(GROUP * Q_BLOCK, HEAD_SIZE)
            keys = k_ref[g, :limit, :]
            scores = dot_t(keys, queries)
            dprob = dot_t(v_ref[g, :limit, :], grads)
            mask = bias[:limit, first:limit]
            probs, dscores = [], []
            for head in range(GROUP):
                cols = slice(head * Q_BLOCK, (head + 1) * Q_BLOCK)
                lse = lse_ref[g * GROUP + head, :, first:limit]
                delta = delta_s[g * GROUP + head, 0:1, first:limit]
                p = jnp.exp(scores[:, cols] + mask - lse)
                probs.append(p.astype(BF))
                dscores.append((p * (dprob[:, cols] - delta)).astype(BF))
            prob = jnp.concatenate(probs, 1)
            dscore = jnp.concatenate(dscores, 1)
            dv_s[g, :limit, :] += jnp.dot(prob, grads, preferred_element_type=F32)
            dqk_s[QUERY_HEADS + g, :limit, :] += jnp.dot(dscore, queries, preferred_element_type=F32)
            dq = dot_0(dscore, keys) * HEAD_SIZE ** (-0.5)
            dqk_s[heads, first:limit, :] = dq.reshape(GROUP, Q_BLOCK, HEAD_SIZE)
        return 0

    lax.fori_loop(0, KEY_VALUE_HEADS, group, 0)
    cosine, sine = cos_ref[...], sin_ref[...]
    for chunk in range(6):
        x = jnp.concatenate([dqk_s[chunk * 2], dqk_s[chunk * 2 + 1]], 1)
        x = x * cosine - turned(x) * sine
        out_ref[:, chunk * 128 : chunk * 128 + 128] = x.astype(BF)
    out_ref[:, 768:896] = jnp.concatenate([dv_s[0], dv_s[1]], 1).astype(BF)
    out_ref[:, 896:960] = dv_s[2].astype(BF)


def vmem(count):
    return [pl.BlockSpec(memory_space=pltpu.VMEM)] * count


def run_forward(qkv, cosine, sine, start):
    tokens = qkv.shape[0]
    shape = jax.ShapeDtypeStruct
    return pl.pallas_call(
        attention_forward,
        out_shape=(
            shape((tokens, 576), BF),
            shape((QUERY_HEADS, tokens, HEAD_SIZE), BF),
            shape((KEY_VALUE_HEADS, tokens, HEAD_SIZE), BF),
            shape((KEY_VALUE_HEADS, tokens, HEAD_SIZE), BF),
            shape((QUERY_HEADS, 1, tokens), F32),
        ),
        in_specs=vmem(4),
        out_specs=tuple(vmem(5)),
        scratch_shapes=[
            pltpu.VMEM((tokens, tokens), F32),
            pltpu.VMEM((QUERY_HEADS, tokens, HEAD_SIZE), F32),
        ],
        compiler_params=pltpu.CompilerParams(vmem_limit_bytes=LIMIT),
        cost_estimate=pl.CostEstimate(flops=6 * 10**9, bytes_accessed=6 * 10**6, transcendentals=4 * 10**6),
        name="attention_forward",
    )(qkv, cosine, sine, start)


def run_backward(q, k, v, lse, att, datt, cosine, sine, start):
    tokens = att.shape[0]
    return pl.pallas_call(
        attention_backward,
        out_shape=jax.ShapeDtypeStruct((tokens, 960), BF),
        in_specs=vmem(9),
        out_specs=vmem(1)[0],
        scratch_shapes=[
            pltpu.VMEM((tokens, tokens), F32),
            pltpu.VMEM((QUERY_HEADS, tokens, HEAD_SIZE), BF),
            pltpu.VMEM((QUERY_HEADS, 8, tokens), F32),
            pltpu.VMEM((QUERY_HEADS + KEY_VALUE_HEADS, tokens, HEAD_SIZE), F32),
            pltpu.VMEM((KEY_VALUE_HEADS, tokens, HEAD_SIZE), F32),
        ],
        compiler_params=pltpu.CompilerParams(vmem_limit_bytes=LIMIT),
        cost_estimate=pl.CostEstimate(flops=12 * 10**9, bytes_accessed=7 * 10**6, transcendentals=4 * 10**6),
        name="attention_backward",
    )(q, k, v, lse, att, datt, cosine, sine, start)


def dot(a, b):
    return jnp.dot(a, b, preferred_element_type=F32)


def forward_layer(hidden_in, weights, tables):
    gain_one, w_qkv, w_o, gain_two, w_gu, w_d = weights
    scale_in = lax.rsqrt(jnp.mean(hidden_in * hidden_in, -1, keepdims=True) + EPS)
    normed = (hidden_in * scale_in * gain_one).astype(BF)
    qkv = dot(normed, w_qkv)
    attended, q, k, v, lse = run_forward(qkv, *tables)
    mixed = hidden_in + dot(attended, w_o)
    scale_mid = lax.rsqrt(jnp.mean(mixed * mixed, -1, keepdims=True) + EPS)
    normed_two = (mixed * scale_mid * gain_two).astype(BF)
    gateup = dot(normed_two, w_gu)
    inner = (jax.nn.silu(gateup[:, :FF]) * gateup[:, FF:]).astype(BF)
    result = mixed + dot(inner, w_d)
    return result, (hidden_in, scale_in, normed, q, k, v, lse, attended, mixed, scale_mid, normed_two, gateup, inner)


def backward_layer(grad_result, weights, tables, kept):
    gain_one, w_qkv, w_o, gain_two, w_gu, w_d = weights
    hidden_in, scale_in, normed, q, k, v, lse, attended, mixed, scale_mid, normed_two, gateup, inner = kept
    grad_low = grad_result.astype(BF)
    grad_wd = dot_0(inner, grad_low).astype(BF)
    grad_inner = dot_t(grad_low, w_d)
    gate = gateup[:, :FF]
    upper = gateup[:, FF:]
    sigma = jax.nn.sigmoid(gate)
    slope = sigma * (1.0 + gate * (1.0 - sigma))
    grad_gateup = jnp.concatenate([grad_inner * upper * slope, grad_inner * gate * sigma], 1).astype(BF)
    grad_wgu = dot_0(normed_two, grad_gateup).astype(BF)
    grad_normed_two = dot_t(grad_gateup, w_gu)
    grad_gain_two = jnp.sum(grad_normed_two * mixed * scale_mid, 0)
    weighted_two = grad_normed_two * gain_two
    grad_mixed = (
        grad_result
        + scale_mid * weighted_two
        - mixed * scale_mid**3 * jnp.mean(weighted_two * mixed, -1, keepdims=True)
    )
    grad_branch = grad_mixed.astype(BF)
    grad_wo = dot_0(attended, grad_branch).astype(BF)
    grad_att = dot_t(grad_branch, w_o).astype(BF)
    grad_qkv = run_backward(q, k, v, lse, attended, grad_att, *tables)
    grad_wqkv = dot_0(normed, grad_qkv).astype(BF)
    grad_normed = dot_t(grad_qkv, w_qkv)
    grad_gain_one = jnp.sum(grad_normed * hidden_in * scale_in, 0)
    weighted_one = grad_normed * gain_one
    grad_input = (
        grad_mixed
        + scale_in * weighted_one
        - hidden_in * scale_in**3 * jnp.mean(weighted_one * hidden_in, -1, keepdims=True)
    )
    return grad_input, (grad_gain_one, grad_wqkv, grad_wo, grad_gain_two, grad_wgu, grad_wd)


BOTH = ("section", "fsdp")


def gather(w):
    full = lax.all_gather(w[0], BOTH, axis=0, tiled=True)
    return full.reshape(2, full.shape[0] // 2, full.shape[1])


def reduce(first, second):
    both = jnp.concatenate([first, second], 0)
    part = lax.psum_scatter(both, BOTH, scatter_dimension=0, tiled=True)
    return lax.psum(part, "replica").astype(F32)[None]


def exchange(section, own_first, own_second):
    at_first = section == 0
    got = lax.ppermute(jnp.where(at_first, own_second, own_first), "section", [(0, 1), (1, 0)])
    keep = jnp.where(at_first, own_first, own_second)
    return jnp.where(at_first, jnp.concatenate([keep, got], 0), jnp.concatenate([got, keep], 0))


def shards(inputs, cotangent, seq_lengths, attn_gain, w_query, key_value_weight, w_out, ffn_gain, w_gateup, w_down):
    section = lax.axis_index("section")
    tokens = inputs.shape[0] // MICRO
    own = lambda array, count: lax.dynamic_slice_in_dim(array, section * count, count, 0)
    gains = gather(jnp.stack([attn_gain[0], ffn_gain[0]], 1)[None])
    qkv_full = gather(jnp.concatenate([w_query, key_value_weight], 2))
    out_full, gateup_full, down_full = gather(w_out), gather(w_gateup), gather(w_down)
    weights = [
        (gains[i, :, 0], qkv_full[i], out_full[i], gains[i, :, 1], gateup_full[i], down_full[i])
        for i in range(2)
    ]
    start, place = positions(own(seq_lengths, 1)[0], tokens)
    tables = rope_tables(place) + (start[None, :],)
    x = own(inputs, tokens)
    cot = own(cotangent, tokens)
    out_one, kept_one = forward_layer(x.astype(F32), weights[0], tables)
    middle = out_one.astype(BF)
    out_two, kept_two = forward_layer(middle.astype(F32), weights[1], tables)
    acts = exchange(section, middle, out_two.astype(BF))
    grad_two, grads_two = backward_layer(cot.astype(F32), weights[1], tables, kept_two)
    low_two = grad_two.astype(BF)
    grad_one, grads_one = backward_layer(low_two.astype(F32), weights[0], tables, kept_one)
    in_grads = exchange(section, grad_one.astype(BF), low_two).astype(F32)
    gain_pair = [jnp.stack([g[0], g[3]], 1).astype(BF) for g in (grads_one, grads_two)]
    gain_sum = reduce(*gain_pair)
    qkv_sum = reduce(grads_one[1], grads_two[1])
    out_sum = reduce(grads_one[2], grads_two[2])
    gateup_sum = reduce(grads_one[4], grads_two[4])
    down_sum = reduce(grads_one[5], grads_two[5])
    return (
        acts[None],
        in_grads[None],
        gain_sum[:, :, 0],
        qkv_sum[:, :, :576],
        qkv_sum[:, :, 576:],
        out_sum,
        gain_sum[:, :, 1],
        gateup_sum,
        down_sum,
    )


def solution(mesh):
    return jax.shard_map(
        shards,
        mesh=mesh,
        in_specs=(
            P(("fsdp", "replica"), None),
            P(("fsdp", "replica"), None),
            P(("fsdp", "replica"), None),
            P("section", "fsdp"),
            P("section", "fsdp", None),
            P("section", "fsdp", None),
            P("section", "fsdp", None),
            P("section", "fsdp"),
            P("section", "fsdp", None),
            P("section", "fsdp", None),
        ),
        out_specs=(
            P("section", ("fsdp", "replica"), None),
            P("section", ("fsdp", "replica"), None),
            P("section", "fsdp"),
            P("section", "fsdp", None),
            P("section", "fsdp", None),
            P("section", "fsdp", None),
            P("section", "fsdp"),
            P("section", "fsdp", None),
            P("section", "fsdp", None),
        ),
        check_vma=False,
    )
```

```python
import functools

import jax
import jax.numpy as jnp
from jax import lax
from jax.experimental import pallas as pl
from jax.experimental.pallas import tpu as pltpu
from jax.sharding import PartitionSpec as P

QUERY_HEADS = 9
KEY_VALUE_HEADS = 3
GROUP = 3
HEAD_SIZE = 64
FF = 1536
MICRO = 2
EPS = 1e-05
ROPE_BASE = 100000.0
Q_BLOCK = 256
LIMIT = 56 * 1024 * 1024
BF = jnp.bfloat16
F32 = jnp.float32


def positions(lengths, token_count):
    ends = jnp.cumsum(lengths)
    index = jnp.arange(token_count, dtype=jnp.int32)
    after = index[:, None] >= ends[None, :]
    start = jnp.sum(jnp.where(after, lengths[None, :], 0), 1)
    return start, index - start


def rope_tables(place):
    half = HEAD_SIZE // 2
    freq = ROPE_BASE ** (-(jnp.arange(half, dtype=F32) * 2.0 / HEAD_SIZE))
    angle = place.astype(F32)[:, None] * freq[None, :]
    cosine, sine = jnp.cos(angle), jnp.sin(angle)
    return (
        jnp.concatenate([cosine] * 4, 1),
        jnp.concatenate([-sine, sine, -sine, sine], 1),
    )


def turned(x):
    lane = lax.broadcasted_iota(jnp.int32, x.shape, 1)
    first = (lane % HEAD_SIZE) < HEAD_SIZE // 2
    return jnp.where(first, pltpu.roll(x, 96, 1), pltpu.roll(x, 32, 1))


def fill_bias(bias, start_ref):
    tokens = bias.shape[0]
    start = start_ref[...]
    for first in range(0, tokens, 128):
        key = lax.broadcasted_iota(jnp.int32, (128, tokens), 0) + first
        query = lax.broadcasted_iota(jnp.int32, (128, tokens), 1)
        ok = (key >= start) & (key <= query)
        bias[first : first + 128, :] = jnp.where(ok, 0.0, -1e30)


def dot_t(a, b):
    return lax.dot_general(a, b, (((1,), (1,)), ((), ())), preferred_element_type=F32)


def dot_0(a, b):
    return lax.dot_general(a, b, (((0,), (0,)), ((), ())), preferred_element_type=F32)


def attention_forward(qkv_ref, cos_ref, sin_ref, start_ref, att_ref, q_ref, k_ref, v_ref, lse_ref, bias, o_s):
    tokens = qkv_ref.shape[0]
    fill_bias(bias, start_ref)
    cosine, sine = cos_ref[...], sin_ref[...]
    for chunk in range(6):
        x = qkv_ref[:, chunk * 128 : chunk * 128 + 128]
        x = x * cosine + turned(x) * sine
        for side in range(2):
            head = chunk * 2 + side
            part = x[:, side * 64 : side * 64 + 64]
            if head < QUERY_HEADS:
                q_ref[head] = (part * HEAD_SIZE ** (-0.5)).astype(BF)
            else:
                k_ref[head - QUERY_HEADS] = part.astype(BF)
    for head in range(KEY_VALUE_HEADS):
        v_ref[head] = qkv_ref[:, 768 + head * 64 : 832 + head * 64].astype(BF)

    def group(g, _):
        for first in range(0, tokens, Q_BLOCK):
            limit = first + Q_BLOCK
            queries = q_ref[pl.ds(g * GROUP, GROUP), first:limit, :].reshape(GROUP * Q_BLOCK, HEAD_SIZE)
            scores = dot_t(k_ref[g, :limit, :], queries)
            mask = bias[:limit, first:limit]
            probs = []
            for head in range(GROUP):
                s = scores[:, head * Q_BLOCK : (head + 1) * Q_BLOCK] + mask
                peak = jnp.max(s, 0, keepdims=True)
                e = jnp.exp(s - peak)
                total = jnp.sum(e, 0, keepdims=True)
                lse_ref[g * GROUP + head, :, first:limit] = peak + jnp.log(total)
                probs.append((e * (1.0 / total)).astype(BF))
            prob = jnp.concatenate(probs, 1)
            out = dot_0(prob, v_ref[g, :limit, :])
            o_s[pl.ds(g * GROUP, GROUP), first:limit, :] = out.reshape(GROUP, Q_BLOCK, HEAD_SIZE)
        return 0

    lax.fori_loop(0, KEY_VALUE_HEADS, group, 0)
    for head in range(0, QUERY_HEADS - 1, 2):
        att_ref[:, head * 64 : head * 64 + 128] = jnp.concatenate([o_s[head], o_s[head + 1]], 1).astype(BF)
    att_ref[:, 512:576] = o_s[8].astype(BF)


def attention_backward(
    q_ref, k_ref, v_ref, lse_ref, att_ref, datt_ref, cos_ref, sin_ref, start_ref, out_ref,
    bias, do_s, delta_s, dqk_s, dv_s,
):
    tokens = att_ref.shape[0]
    fill_bias(bias, start_ref)
    ones = jnp.ones((8, HEAD_SIZE), BF)
    for head in range(QUERY_HEADS):
        cols = slice(head * 64, head * 64 + 64)
        grad = datt_ref[:, cols]
        do_s[head] = grad
        product = (grad.astype(F32) * att_ref[:, cols].astype(F32)).astype(BF)
        delta_s[head] = dot_t(ones, product)
    dqk_s[QUERY_HEADS:] = jnp.zeros((KEY_VALUE_HEADS, tokens, HEAD_SIZE), F32)
    dv_s[...] = jnp.zeros_like(dv_s)

    def group(g, _):
        for first in range(0, tokens, Q_BLOCK):
            limit = first + Q_BLOCK
            heads = pl.ds(g * GROUP, GROUP)
            queries = q_ref[heads, first:limit, :].reshape(GROUP * Q_BLOCK, HEAD_SIZE)
            grads = do_s[heads, first:limit, :].reshape(GROUP * Q_BLOCK, HEAD_SIZE)
            keys = k_ref[g, :limit, :]
            scores = dot_t(keys, queries)
            dprob = dot_t(v_ref[g, :limit, :], grads)
            mask = bias[:limit, first:limit]
            probs, dscores = [], []
            for head in range(GROUP):
                cols = slice(head * Q_BLOCK, (head + 1) * Q_BLOCK)
                lse = lse_ref[g * GROUP + head, :, first:limit]
                delta = delta_s[g * GROUP + head, 0:1, first:limit]
                p = jnp.exp(scores[:, cols] + mask - lse)
                probs.append(p.astype(BF))
                dscores.append((p * (dprob[:, cols] - delta)).astype(BF))
            prob = jnp.concatenate(probs, 1)
            dscore = jnp.concatenate(dscores, 1)
            dv_s[g, :limit, :] += jnp.dot(prob, grads, preferred_element_type=F32)
            dqk_s[QUERY_HEADS + g, :limit, :] += jnp.dot(dscore, queries, preferred_element_type=F32)
            dq = dot_0(dscore, keys) * HEAD_SIZE ** (-0.5)
            dqk_s[heads, first:limit, :] = dq.reshape(GROUP, Q_BLOCK, HEAD_SIZE)
        return 0

    lax.fori_loop(0, KEY_VALUE_HEADS, group, 0)
    cosine, sine = cos_ref[...], sin_ref[...]
    for chunk in range(6):
        x = jnp.concatenate([dqk_s[chunk * 2], dqk_s[chunk * 2 + 1]], 1)
        x = x * cosine - turned(x) * sine
        out_ref[:, chunk * 128 : chunk * 128 + 128] = x.astype(BF)
    out_ref[:, 768:896] = jnp.concatenate([dv_s[0], dv_s[1]], 1).astype(BF)
    out_ref[:, 896:960] = dv_s[2].astype(BF)


def vmem(count):
    return [pl.BlockSpec(memory_space=pltpu.VMEM)] * count


def run_forward(qkv, cosine, sine, start):
    tokens = qkv.shape[0]
    shape = jax.ShapeDtypeStruct
    return pl.pallas_call(
        attention_forward,
        out_shape=(
            shape((tokens, 576), BF),
            shape((QUERY_HEADS, tokens, HEAD_SIZE), BF),
            shape((KEY_VALUE_HEADS, tokens, HEAD_SIZE), BF),
            shape((KEY_VALUE_HEADS, tokens, HEAD_SIZE), BF),
            shape((QUERY_HEADS, 1, tokens), F32),
        ),
        in_specs=vmem(4),
        out_specs=tuple(vmem(5)),
        scratch_shapes=[
            pltpu.VMEM((tokens, tokens), F32),
            pltpu.VMEM((QUERY_HEADS, tokens, HEAD_SIZE), F32),
        ],
        compiler_params=pltpu.CompilerParams(vmem_limit_bytes=LIMIT),
        cost_estimate=pl.CostEstimate(flops=6 * 10**9, bytes_accessed=6 * 10**6, transcendentals=4 * 10**6),
        name="attention_forward",
    )(qkv, cosine, sine, start)


def run_backward(q, k, v, lse, att, datt, cosine, sine, start):
    tokens = att.shape[0]
    return pl.pallas_call(
        attention_backward,
        out_shape=jax.ShapeDtypeStruct((tokens, 960), BF),
        in_specs=vmem(9),
        out_specs=vmem(1)[0],
        scratch_shapes=[
            pltpu.VMEM((tokens, tokens), F32),
            pltpu.VMEM((QUERY_HEADS, tokens, HEAD_SIZE), BF),
            pltpu.VMEM((QUERY_HEADS, 8, tokens), F32),
            pltpu.VMEM((QUERY_HEADS + KEY_VALUE_HEADS, tokens, HEAD_SIZE), F32),
            pltpu.VMEM((KEY_VALUE_HEADS, tokens, HEAD_SIZE), F32),
        ],
        compiler_params=pltpu.CompilerParams(vmem_limit_bytes=LIMIT),
        cost_estimate=pl.CostEstimate(flops=12 * 10**9, bytes_accessed=7 * 10**6, transcendentals=4 * 10**6),
        name="attention_backward",
    )(q, k, v, lse, att, datt, cosine, sine, start)


def dot(a, b):
    return jnp.dot(a, b, preferred_element_type=F32)


def forward_layer(hidden_in, weights, tables):
    gain_one, w_qkv, w_o, gain_two, w_gu, w_d = weights
    scale_in = lax.rsqrt(jnp.mean(hidden_in * hidden_in, -1, keepdims=True) + EPS)
    normed = (hidden_in * scale_in * gain_one).astype(BF)
    qkv = dot(normed, w_qkv)
    attended, q, k, v, lse = run_forward(qkv, *tables)
    mixed = hidden_in + dot(attended, w_o)
    scale_mid = lax.rsqrt(jnp.mean(mixed * mixed, -1, keepdims=True) + EPS)
    normed_two = (mixed * scale_mid * gain_two).astype(BF)
    gateup = dot(normed_two, w_gu)
    inner = (jax.nn.silu(gateup[:, :FF]) * gateup[:, FF:]).astype(BF)
    result = mixed + dot(inner, w_d)
    return result, (hidden_in, scale_in, normed, q, k, v, lse, attended, mixed, scale_mid, normed_two, gateup, inner)


def backward_layer(grad_result, weights, tables, kept):
    gain_one, w_qkv, w_o, gain_two, w_gu, w_d = weights
    hidden_in, scale_in, normed, q, k, v, lse, attended, mixed, scale_mid, normed_two, gateup, inner = kept
    grad_low = grad_result.astype(BF)
    grad_wd = dot_0(inner, grad_low).astype(BF)
    grad_inner = dot_t(grad_low, w_d)
    gate = gateup[:, :FF]
    upper = gateup[:, FF:]
    sigma = jax.nn.sigmoid(gate)
    slope = sigma * (1.0 + gate * (1.0 - sigma))
    grad_gateup = jnp.concatenate([grad_inner * upper * slope, grad_inner * gate * sigma], 1).astype(BF)
    grad_wgu = dot_0(normed_two, grad_gateup).astype(BF)
    grad_normed_two = dot_t(grad_gateup, w_gu)
    grad_gain_two = jnp.sum(grad_normed_two * mixed * scale_mid, 0)
    weighted_two = grad_normed_two * gain_two
    grad_mixed = (
        grad_result
        + scale_mid * weighted_two
        - mixed * scale_mid**3 * jnp.mean(weighted_two * mixed, -1, keepdims=True)
    )
    grad_branch = grad_mixed.astype(BF)
    grad_wo = dot_0(attended, grad_branch).astype(BF)
    grad_att = dot_t(grad_branch, w_o).astype(BF)
    grad_qkv = run_backward(q, k, v, lse, attended, grad_att, *tables)
    grad_wqkv = dot_0(normed, grad_qkv).astype(BF)
    grad_normed = dot_t(grad_qkv, w_qkv)
    grad_gain_one = jnp.sum(grad_normed * hidden_in * scale_in, 0)
    weighted_one = grad_normed * gain_one
    grad_input = (
        grad_mixed
        + scale_in * weighted_one
        - hidden_in * scale_in**3 * jnp.mean(weighted_one * hidden_in, -1, keepdims=True)
    )
    return grad_input, (grad_gain_one, grad_wqkv, grad_wo, grad_gain_two, grad_wgu, grad_wd)


SWAP = [(0, 1), (1, 0)]


def assemble_kernel(*refs):
    pieces, full, sems = refs[:8], refs[8], refs[9]
    section = lax.axis_index("section")
    own = lax.axis_index("fsdp")
    copies = []
    for core in range(2):
        half = (section + core) % 2
        for step in range(4):
            low = (own % 2 + step % 2) % 2
            high = (own // 2 + step // 2) % 2
            at = core * 4 + step
            copies.append(pltpu.make_async_copy(pieces[at], full.at[high * 2 + low, half], sems.at[at]))
    for copy in copies:
        copy.start()
    for copy in copies:
        copy.wait()


def assemble(pieces):
    rows, columns = pieces[0].shape
    full = pl.pallas_call(
        assemble_kernel,
        out_shape=jax.ShapeDtypeStruct((4, 2, rows, columns), BF),
        in_specs=[pl.BlockSpec(memory_space=pl.ANY)] * 8,
        out_specs=pl.BlockSpec(memory_space=pl.ANY),
        scratch_shapes=[pltpu.SemaphoreType.DMA((8,))],
        compiler_params=pltpu.CompilerParams(vmem_limit_bytes=LIMIT),
        cost_estimate=pl.CostEstimate(flops=0, bytes_accessed=32 * rows * columns, transcendentals=0),
        name="assemble",
    )(*pieces)
    return full.reshape(8 * rows, columns)


def peer(value, step):
    return lax.ppermute(value, "fsdp", [(i, i ^ step) for i in range(4)])


def swap(value):
    return lax.ppermute(value, "section", SWAP)


def gather(section, packs):
    at_first = section == 0
    halves = [[], []]
    for pack in packs:
        parts = pack.reshape(2, pack.shape[0] // 2, pack.shape[1])
        keep = jnp.where(at_first, parts[0], parts[1])
        got = swap(jnp.where(at_first, parts[1], parts[0]))
        halves[0].append(jnp.where(at_first, keep, got))
        halves[1].append(jnp.where(at_first, got, keep))
    order = halves[0] + halves[1]
    arrived = []
    full = []
    for at, half in enumerate(order):
        if at >= 2:
            half = lax.optimization_barrier((half, arrived[at - 2]))[0]
        pieces = [half] + [peer(half, step) for step in (3, 1, 2)]
        pieces = [pieces[0], pieces[2], pieces[3], pieces[1]]
        arrived.append(pieces[1:])
        full.append(assemble(pieces + [swap(piece) for piece in pieces]))
    return full[: len(packs)], full[len(packs) :]


def replica_sum(own):
    count = lax.axis_size("replica")
    if count != 4:
        return lax.psum(own.astype(BF), "replica").astype(F32)
    send = lambda value, pairs: lax.ppermute(value.astype(BF), "replica", pairs).astype(F32)
    one = send(own, [(0, 1), (3, 2)])
    two = send(own + one, [(1, 2), (2, 1)])
    three = send(own + two, [(2, 3), (1, 0)])
    return own + one + two + three


def reduce(section, grad):
    own = lax.axis_index("fsdp")
    rows, columns = grad.shape[0] // 8, grad.shape[1]
    parts = grad.reshape(4, 2, rows, columns)
    pick = lambda half: lax.dynamic_slice_in_dim(parts, half, 1, 1)[:, 0]
    half = (pick(section).astype(F32) + swap(pick(1 - section)).astype(F32)).astype(BF)
    block = lambda at: lax.dynamic_slice_in_dim(half, at, 1, 0)[0]
    total = block(own).astype(F32)
    for step in (3, 1, 2):
        total = total + peer(block(own ^ step), step).astype(F32)
    return replica_sum(total).astype(BF)


def finish(section, first, second):
    at_first = section == 0
    got = swap(jnp.where(at_first, second, first))
    keep = jnp.where(at_first, first, second)
    low, high = jnp.where(at_first, keep, got), jnp.where(at_first, got, keep)
    return jnp.concatenate([low, high], 0).astype(F32)[None]


def exchange(section, own_first, own_second):
    at_first = section == 0
    got = lax.ppermute(jnp.where(at_first, own_second, own_first), "section", [(0, 1), (1, 0)])
    keep = jnp.where(at_first, own_first, own_second)
    return jnp.where(at_first, jnp.concatenate([keep, got], 0), jnp.concatenate([got, keep], 0))


def shards(inputs, cotangent, seq_lengths, attn_gain, w_query, key_value_weight, w_out, ffn_gain, w_gateup, w_down):
    section = lax.axis_index("section")
    tokens = inputs.shape[0] // MICRO
    own = lambda array, count: lax.dynamic_slice_in_dim(array, section * count, count, 0)
    pad = lambda rows: jnp.zeros((rows, 126), BF)
    mixed_pack = jnp.concatenate(
        [w_query[0], key_value_weight[0], w_out[0], attn_gain[0][:, None], ffn_gain[0][:, None], pad(w_out.shape[1])], 1
    )
    weights = [
        (a[:, 1536], a[:, :960], a[:, 960:1536], a[:, 1537], gu, down)
        for a, gu, down in gather(section, [mixed_pack, w_gateup[0], w_down[0]])
    ]
    start, place = positions(own(seq_lengths, 1)[0], tokens)
    tables = rope_tables(place) + (start[None, :],)
    x = own(inputs, tokens)
    cot = own(cotangent, tokens)
    out_one, kept_one = forward_layer(x.astype(F32), weights[0], tables)
    middle = out_one.astype(BF)
    out_two, kept_two = forward_layer(middle.astype(F32), weights[1], tables)
    acts = exchange(section, middle, out_two.astype(BF))
    grad_two, grads_two = backward_layer(cot.astype(F32), weights[1], tables, kept_two)
    low_two = grad_two.astype(BF)
    grad_one, grads_one = backward_layer(low_two.astype(F32), weights[0], tables, kept_one)
    in_grads = exchange(section, grad_one.astype(BF), low_two).astype(F32)
    sums = []
    for gain_one, g_qkv, g_out, gain_two, g_gateup, g_down in (grads_two, grads_one):
        gains = [gain_one.astype(BF)[:, None], gain_two.astype(BF)[:, None], pad(g_qkv.shape[0])]
        mixed = jnp.concatenate([g_qkv, g_out] + gains, 1)
        sums.append([reduce(section, g) for g in (g_down, g_gateup, mixed)])
    down_sum, gateup_sum, mixed_sum = [finish(section, b, a) for a, b in zip(*sums)]
    return (
        acts[None],
        in_grads[None],
        mixed_sum[:, :, 1536],
        mixed_sum[:, :, :576],
        mixed_sum[:, :, 576:960],
        mixed_sum[:, :, 960:1536],
        mixed_sum[:, :, 1537],
        gateup_sum,
        down_sum,
    )


def solution(mesh):
    return jax.shard_map(
        shards,
        mesh=mesh,
        in_specs=(
            P(("fsdp", "replica"), None),
            P(("fsdp", "replica"), None),
            P(("fsdp", "replica"), None),
            P("section", "fsdp"),
            P("section", "fsdp", None),
            P("section", "fsdp", None),
            P("section", "fsdp", None),
            P("section", "fsdp"),
            P("section", "fsdp", None),
            P("section", "fsdp", None),
        ),
        out_specs=(
            P("section", ("fsdp", "replica"), None),
            P("section", ("fsdp", "replica"), None),
            P("section", "fsdp"),
            P("section", "fsdp", None),
            P("section", "fsdp", None),
            P("section", "fsdp", None),
            P("section", "fsdp"),
            P("section", "fsdp", None),
            P("section", "fsdp", None),
        ),
        check_vma=False,
    )
```

```python
import functools

import jax
import jax.numpy as jnp
from jax import lax
from jax.experimental import pallas as pl
from jax.experimental.pallas import tpu as pltpu
from jax.sharding import PartitionSpec as P

QUERY_HEADS = 9
KEY_VALUE_HEADS = 3
GROUP = 3
HEAD_SIZE = 64
FF = 1536
MICRO = 2
EPS = 1e-05
ROPE_BASE = 100000.0
Q_BLOCK = 256
LIMIT = 56 * 1024 * 1024
BF = jnp.bfloat16
F32 = jnp.float32


def positions(lengths, token_count):
    ends = jnp.cumsum(lengths)
    index = jnp.arange(token_count, dtype=jnp.int32)
    after = index[:, None] >= ends[None, :]
    start = jnp.sum(jnp.where(after, lengths[None, :], 0), 1)
    return start, index - start


def rope_tables(place):
    half = HEAD_SIZE // 2
    freq = ROPE_BASE ** (-(jnp.arange(half, dtype=F32) * 2.0 / HEAD_SIZE))
    angle = place.astype(F32)[:, None] * freq[None, :]
    cosine, sine = jnp.cos(angle), jnp.sin(angle)
    return (
        jnp.concatenate([cosine] * 4, 1),
        jnp.concatenate([-sine, sine, -sine, sine], 1),
    )


def turned(x):
    lane = lax.broadcasted_iota(jnp.int32, x.shape, 1)
    first = (lane % HEAD_SIZE) < HEAD_SIZE // 2
    return jnp.where(first, pltpu.roll(x, 96, 1), pltpu.roll(x, 32, 1))


def fill_bias(bias, start_ref):
    tokens = bias.shape[0]
    start = start_ref[...]
    for first in range(0, tokens, 128):
        key = lax.broadcasted_iota(jnp.int32, (128, tokens), 0) + first
        query = lax.broadcasted_iota(jnp.int32, (128, tokens), 1)
        ok = (key >= start) & (key <= query)
        bias[first : first + 128, :] = jnp.where(ok, 0.0, -1e30)


def dot_t(a, b):
    return lax.dot_general(a, b, (((1,), (1,)), ((), ())), preferred_element_type=F32)


def dot_0(a, b):
    return lax.dot_general(a, b, (((0,), (0,)), ((), ())), preferred_element_type=F32)


def attention_forward(qkv_ref, cos_ref, sin_ref, start_ref, att_ref, q_ref, k_ref, v_ref, lse_ref, bias, o_s):
    tokens = qkv_ref.shape[0]
    fill_bias(bias, start_ref)
    cosine, sine = cos_ref[...], sin_ref[...]
    for chunk in range(6):
        x = qkv_ref[:, chunk * 128 : chunk * 128 + 128]
        x = x * cosine + turned(x) * sine
        for side in range(2):
            head = chunk * 2 + side
            part = x[:, side * 64 : side * 64 + 64]
            if head < QUERY_HEADS:
                q_ref[head] = (part * HEAD_SIZE ** (-0.5)).astype(BF)
            else:
                k_ref[head - QUERY_HEADS] = part.astype(BF)
    for head in range(KEY_VALUE_HEADS):
        v_ref[head] = qkv_ref[:, 768 + head * 64 : 832 + head * 64].astype(BF)

    def group(g, _):
        for first in range(0, tokens, Q_BLOCK):
            limit = first + Q_BLOCK
            queries = q_ref[pl.ds(g * GROUP, GROUP), first:limit, :].reshape(GROUP * Q_BLOCK, HEAD_SIZE)
            scores = dot_t(k_ref[g, :limit, :], queries)
            mask = bias[:limit, first:limit]
            probs = []
            for head in range(GROUP):
                s = scores[:, head * Q_BLOCK : (head + 1) * Q_BLOCK] + mask
                peak = jnp.max(s, 0, keepdims=True)
                e = jnp.exp(s - peak)
                total = jnp.sum(e, 0, keepdims=True)
                lse_ref[g * GROUP + head, :, first:limit] = peak + jnp.log(total)
                probs.append((e * (1.0 / total)).astype(BF))
            prob = jnp.concatenate(probs, 1)
            out = dot_0(prob, v_ref[g, :limit, :])
            o_s[pl.ds(g * GROUP, GROUP), first:limit, :] = out.reshape(GROUP, Q_BLOCK, HEAD_SIZE)
        return 0

    lax.fori_loop(0, KEY_VALUE_HEADS, group, 0)
    for head in range(0, QUERY_HEADS - 1, 2):
        att_ref[:, head * 64 : head * 64 + 128] = jnp.concatenate([o_s[head], o_s[head + 1]], 1).astype(BF)
    att_ref[:, 512:576] = o_s[8].astype(BF)


def attention_backward(
    q_ref, k_ref, v_ref, lse_ref, att_ref, datt_ref, cos_ref, sin_ref, start_ref, out_ref,
    bias, do_s, delta_s, dqk_s, dv_s,
):
    tokens = att_ref.shape[0]
    fill_bias(bias, start_ref)
    ones = jnp.ones((8, HEAD_SIZE), BF)
    for head in range(QUERY_HEADS):
        cols = slice(head * 64, head * 64 + 64)
        grad = datt_ref[:, cols]
        do_s[head] = grad
        product = (grad.astype(F32) * att_ref[:, cols].astype(F32)).astype(BF)
        delta_s[head] = dot_t(ones, product)
    dqk_s[QUERY_HEADS:] = jnp.zeros((KEY_VALUE_HEADS, tokens, HEAD_SIZE), F32)
    dv_s[...] = jnp.zeros_like(dv_s)

    def group(g, _):
        for first in range(0, tokens, Q_BLOCK):
            limit = first + Q_BLOCK
            heads = pl.ds(g * GROUP, GROUP)
            queries = q_ref[heads, first:limit, :].reshape(GROUP * Q_BLOCK, HEAD_SIZE)
            grads = do_s[heads, first:limit, :].reshape(GROUP * Q_BLOCK, HEAD_SIZE)
            keys = k_ref[g, :limit, :]
            scores = dot_t(keys, queries)
            dprob = dot_t(v_ref[g, :limit, :], grads)
            mask = bias[:limit, first:limit]
            probs, dscores = [], []
            for head in range(GROUP):
                cols = slice(head * Q_BLOCK, (head + 1) * Q_BLOCK)
                lse = lse_ref[g * GROUP + head, :, first:limit]
                delta = delta_s[g * GROUP + head, 0:1, first:limit]
                p = jnp.exp(scores[:, cols] + mask - lse)
                probs.append(p.astype(BF))
                dscores.append((p * (dprob[:, cols] - delta)).astype(BF))
            prob = jnp.concatenate(probs, 1)
            dscore = jnp.concatenate(dscores, 1)
            dv_s[g, :limit, :] += jnp.dot(prob, grads, preferred_element_type=F32)
            dqk_s[QUERY_HEADS + g, :limit, :] += jnp.dot(dscore, queries, preferred_element_type=F32)
            dq = dot_0(dscore, keys) * HEAD_SIZE ** (-0.5)
            dqk_s[heads, first:limit, :] = dq.reshape(GROUP, Q_BLOCK, HEAD_SIZE)
        return 0

    lax.fori_loop(0, KEY_VALUE_HEADS, group, 0)
    cosine, sine = cos_ref[...], sin_ref[...]
    for chunk in range(6):
        x = jnp.concatenate([dqk_s[chunk * 2], dqk_s[chunk * 2 + 1]], 1)
        x = x * cosine - turned(x) * sine
        out_ref[:, chunk * 128 : chunk * 128 + 128] = x.astype(BF)
    out_ref[:, 768:896] = jnp.concatenate([dv_s[0], dv_s[1]], 1).astype(BF)
    out_ref[:, 896:960] = dv_s[2].astype(BF)


def vmem(count):
    return [pl.BlockSpec(memory_space=pltpu.VMEM)] * count


def run_forward(qkv, cosine, sine, start):
    tokens = qkv.shape[0]
    shape = jax.ShapeDtypeStruct
    return pl.pallas_call(
        attention_forward,
        out_shape=(
            shape((tokens, 576), BF),
            shape((QUERY_HEADS, tokens, HEAD_SIZE), BF),
            shape((KEY_VALUE_HEADS, tokens, HEAD_SIZE), BF),
            shape((KEY_VALUE_HEADS, tokens, HEAD_SIZE), BF),
            shape((QUERY_HEADS, 1, tokens), F32),
        ),
        in_specs=vmem(4),
        out_specs=tuple(vmem(5)),
        scratch_shapes=[
            pltpu.VMEM((tokens, tokens), F32),
            pltpu.VMEM((QUERY_HEADS, tokens, HEAD_SIZE), F32),
        ],
        compiler_params=pltpu.CompilerParams(vmem_limit_bytes=LIMIT),
        cost_estimate=pl.CostEstimate(flops=6 * 10**9, bytes_accessed=6 * 10**6, transcendentals=4 * 10**6),
        name="attention_forward",
    )(qkv, cosine, sine, start)


def run_backward(q, k, v, lse, att, datt, cosine, sine, start):
    tokens = att.shape[0]
    return pl.pallas_call(
        attention_backward,
        out_shape=jax.ShapeDtypeStruct((tokens, 960), BF),
        in_specs=vmem(9),
        out_specs=vmem(1)[0],
        scratch_shapes=[
            pltpu.VMEM((tokens, tokens), F32),
            pltpu.VMEM((QUERY_HEADS, tokens, HEAD_SIZE), BF),
            pltpu.VMEM((QUERY_HEADS, 8, tokens), F32),
            pltpu.VMEM((QUERY_HEADS + KEY_VALUE_HEADS, tokens, HEAD_SIZE), F32),
            pltpu.VMEM((KEY_VALUE_HEADS, tokens, HEAD_SIZE), F32),
        ],
        compiler_params=pltpu.CompilerParams(vmem_limit_bytes=LIMIT),
        cost_estimate=pl.CostEstimate(flops=12 * 10**9, bytes_accessed=7 * 10**6, transcendentals=4 * 10**6),
        name="attention_backward",
    )(q, k, v, lse, att, datt, cosine, sine, start)


def dot(a, b):
    return jnp.dot(a, b, preferred_element_type=F32)


def forward_layer(hidden_in, weights, tables):
    gain_one, w_qkv, w_o, gain_two, w_gu, w_d = weights
    scale_in = lax.rsqrt(jnp.mean(hidden_in * hidden_in, -1, keepdims=True) + EPS)
    normed = (hidden_in * scale_in * gain_one).astype(BF)
    qkv = dot(normed, w_qkv)
    attended, q, k, v, lse = run_forward(qkv, *tables)
    mixed = hidden_in + dot(attended, w_o)
    scale_mid = lax.rsqrt(jnp.mean(mixed * mixed, -1, keepdims=True) + EPS)
    normed_two = (mixed * scale_mid * gain_two).astype(BF)
    gateup = dot(normed_two, w_gu)
    inner = (jax.nn.silu(gateup[:, :FF]) * gateup[:, FF:]).astype(BF)
    result = mixed + dot(inner, w_d)
    return result, (hidden_in, scale_in, normed, q, k, v, lse, attended, mixed, scale_mid, normed_two, gateup, inner)


def backward_ffn(grad_result, weights, kept):
    gain_one, w_qkv, w_o, gain_two, w_gu, w_d = weights
    hidden_in, scale_in, normed, q, k, v, lse, attended, mixed, scale_mid, normed_two, gateup, inner = kept
    grad_low = grad_result.astype(BF)
    grad_wd = dot_0(inner, grad_low).astype(BF)
    grad_inner = dot_t(grad_low, w_d)
    gate = gateup[:, :FF]
    upper = gateup[:, FF:]
    sigma = jax.nn.sigmoid(gate)
    slope = sigma * (1.0 + gate * (1.0 - sigma))
    grad_gateup = jnp.concatenate([grad_inner * upper * slope, grad_inner * gate * sigma], 1).astype(BF)
    grad_wgu = dot_0(normed_two, grad_gateup).astype(BF)
    grad_normed_two = dot_t(grad_gateup, w_gu)
    grad_gain_two = jnp.sum(grad_normed_two * mixed * scale_mid, 0)
    weighted_two = grad_normed_two * gain_two
    grad_mixed = (
        grad_result
        + scale_mid * weighted_two
        - mixed * scale_mid**3 * jnp.mean(weighted_two * mixed, -1, keepdims=True)
    )
    grad_branch = grad_mixed.astype(BF)
    grad_wo = dot_0(attended, grad_branch).astype(BF)
    grad_att = dot_t(grad_branch, w_o).astype(BF)
    return grad_mixed, grad_att, grad_wo, grad_gain_two, grad_wgu, grad_wd


def backward_attention(grad_att, kept, tables):
    hidden_in, scale_in, normed, q, k, v, lse, attended = kept[:8]
    return run_backward(q, k, v, lse, attended, grad_att, *tables)


def backward_input(grad_mixed, grad_qkv, weights, kept):
    gain_one, w_qkv = weights[:2]
    hidden_in, scale_in, normed = kept[:3]
    grad_wqkv = dot_0(normed, grad_qkv).astype(BF)
    grad_normed = dot_t(grad_qkv, w_qkv)
    grad_gain_one = jnp.sum(grad_normed * hidden_in * scale_in, 0)
    weighted_one = grad_normed * gain_one
    grad_input = (
        grad_mixed
        + scale_in * weighted_one
        - hidden_in * scale_in**3 * jnp.mean(weighted_one * hidden_in, -1, keepdims=True)
    )
    return grad_input, grad_wqkv, grad_gain_one


SWAP = [(0, 1), (1, 0)]


def assemble_kernel(*refs):
    pieces, full = refs[:8], refs[8]
    section = lax.axis_index("section")
    own = lax.axis_index("fsdp")
    for core in range(2):
        half = (section + core) % 2
        for step in range(4):
            low = (own % 2 + step % 2) % 2
            high = (own // 2 + step // 2) % 2
            full[high * 2 + low, half] = pieces[core * 4 + step][...]


def assemble(pieces):
    rows, columns = pieces[0].shape
    full = pl.pallas_call(
        assemble_kernel,
        out_shape=jax.ShapeDtypeStruct((4, 2, rows, columns), BF),
        in_specs=vmem(8),
        out_specs=vmem(1)[0],
        compiler_params=pltpu.CompilerParams(vmem_limit_bytes=24 * 1024 * 1024),
        cost_estimate=pl.CostEstimate(flops=0, bytes_accessed=32 * rows * columns, transcendentals=0),
        name="assemble",
    )(*pieces)
    return full.reshape(8 * rows, columns)


def peer(value, step):
    return lax.ppermute(value, "fsdp", [(i, i ^ step) for i in range(4)])


def swap(value):
    return lax.ppermute(value, "section", SWAP)


def gather(section, packs):
    at_first = section == 0
    halves = [[], []]
    for pack in packs:
        parts = pack.reshape(2, pack.shape[0] // 2, pack.shape[1])
        keep = jnp.where(at_first, parts[0], parts[1])
        got = swap(jnp.where(at_first, parts[1], parts[0]))
        halves[0].append(jnp.where(at_first, keep, got))
        halves[1].append(jnp.where(at_first, got, keep))
    order = halves[0] + halves[1]
    arrived = []
    full = []
    for at, half in enumerate(order):
        if at >= 2:
            half = lax.optimization_barrier((half, arrived[at - 2]))[0]
        pieces = [half] + [peer(half, step) for step in (3, 1, 2)]
        pieces = [pieces[0], pieces[2], pieces[3], pieces[1]]
        arrived.append(pieces[1:])
        full.append(assemble(pieces + [swap(piece) for piece in pieces]))
    return full[: len(packs)], full[len(packs) :]


def replica_sum(own):
    count = lax.axis_size("replica")
    if count != 4:
        return lax.psum(own.astype(BF), "replica").astype(F32)
    send = lambda value, pairs: lax.ppermute(value.astype(BF), "replica", pairs).astype(F32)
    one = send(own, [(0, 1), (3, 2)])
    two = send(own + one, [(1, 2), (2, 1)])
    three = send(own + two, [(2, 3), (1, 0)])
    return own + one + two + three


def core_sum(section, grad):
    rows, columns = grad.shape[0] // 8, grad.shape[1]
    parts = grad.reshape(4, 2, rows, columns)
    pick = lambda half: lax.dynamic_slice_in_dim(parts, half, 1, 1)[:, 0]
    return (pick(section).astype(F32) + swap(pick(1 - section)).astype(F32)).astype(BF)


def fsdp_sum(half):
    own = lax.axis_index("fsdp")
    block = lambda at: lax.dynamic_slice_in_dim(half, at, 1, 0)[0]
    total = block(own).astype(F32)
    for step in (3, 1, 2):
        total = total + peer(block(own ^ step), step).astype(F32)
    return total


def tie(value, *others):
    return lax.optimization_barrier((value,) + others)


def finish(section, first, second):
    at_first = section == 0
    got = swap(jnp.where(at_first, second, first))
    keep = jnp.where(at_first, first, second)
    low, high = jnp.where(at_first, keep, got), jnp.where(at_first, got, keep)
    return jnp.concatenate([low, high], 0).astype(F32)[None]


def exchange(section, own_first, own_second):
    at_first = section == 0
    got = lax.ppermute(jnp.where(at_first, own_second, own_first), "section", [(0, 1), (1, 0)])
    keep = jnp.where(at_first, own_first, own_second)
    return jnp.where(at_first, jnp.concatenate([keep, got], 0), jnp.concatenate([got, keep], 0))


def shards(inputs, cotangent, seq_lengths, attn_gain, w_query, key_value_weight, w_out, ffn_gain, w_gateup, w_down):
    section = lax.axis_index("section")
    tokens = inputs.shape[0] // MICRO
    own = lambda array, count: lax.dynamic_slice_in_dim(array, section * count, count, 0)
    pad = lambda rows: jnp.zeros((rows, 126), BF)
    mixed_pack = jnp.concatenate(
        [w_query[0], key_value_weight[0], w_out[0], attn_gain[0][:, None], ffn_gain[0][:, None], pad(w_out.shape[1])], 1
    )
    weights = [
        (a[:, 1536], a[:, :960], a[:, 960:1536], a[:, 1537], gu, down)
        for a, gu, down in gather(section, [mixed_pack, w_gateup[0], w_down[0]])
    ]
    start, place = positions(own(seq_lengths, 1)[0], tokens)
    tables = rope_tables(place) + (start[None, :],)
    x = own(inputs, tokens)
    cot = own(cotangent, tokens)
    out_one, kept_one = forward_layer(x.astype(F32), weights[0], tables)
    middle = out_one.astype(BF)
    out_two, kept_two = forward_layer(middle.astype(F32), weights[1], tables)
    acts = exchange(section, middle, out_two.astype(BF))
    def pack_grads(g_qkv, g_out, gain_one, gain_two):
        columns = [gain_one.astype(BF)[:, None], gain_two.astype(BF)[:, None], pad(g_qkv.shape[0])]
        return jnp.concatenate([g_qkv, g_out] + columns, 1)

    dmixed, datt, g_out, gain_two, g_gateup, g_down = backward_ffn(cot.astype(F32), weights[1], kept_two)
    down_b, gateup_b = core_sum(section, g_down), core_sum(section, g_gateup)
    dqkv, down_b, gateup_b = tie(backward_attention(datt, kept_two, tables), down_b, gateup_b)
    grad_two, g_qkv, gain_one = backward_input(dmixed, dqkv, weights[1], kept_two)
    mixed_b = core_sum(section, pack_grads(g_qkv, g_out, gain_one, gain_two))
    low_two = grad_two.astype(BF)
    down_b, gateup_b = fsdp_sum(down_b), fsdp_sum(gateup_b)
    dmixed, datt, g_out, gain_two, g_gateup, g_down = backward_ffn(low_two.astype(F32), weights[0], kept_one)
    datt, down_b, gateup_b, mixed_b = tie(datt, down_b, gateup_b, mixed_b)
    down_a, gateup_a = core_sum(section, g_down), core_sum(section, g_gateup)
    mixed_b = fsdp_sum(mixed_b)
    dqkv = backward_attention(datt, kept_one, tables)
    dqkv, down_a, gateup_a, mixed_b = tie(dqkv, down_a, gateup_a, mixed_b)
    grad_one, g_qkv, gain_one = backward_input(dmixed, dqkv, weights[0], kept_one)
    in_grads = exchange(section, grad_one.astype(BF), low_two).astype(F32)
    mixed_a = core_sum(section, pack_grads(g_qkv, g_out, gain_one, gain_two))
    sums = [
        [replica_sum(part).astype(BF) for part in (down_b, gateup_b, mixed_b)],
        [replica_sum(fsdp_sum(part)).astype(BF) for part in (down_a, gateup_a, mixed_a)],
    ]
    down_sum, gateup_sum, mixed_sum = [finish(section, b, a) for a, b in zip(*sums)]
    return (
        acts[None],
        in_grads[None],
        mixed_sum[:, :, 1536],
        mixed_sum[:, :, :576],
        mixed_sum[:, :, 576:960],
        mixed_sum[:, :, 960:1536],
        mixed_sum[:, :, 1537],
        gateup_sum,
        down_sum,
    )


def solution(mesh):
    return jax.shard_map(
        shards,
        mesh=mesh,
        in_specs=(
            P(("fsdp", "replica"), None),
            P(("fsdp", "replica"), None),
            P(("fsdp", "replica"), None),
            P("section", "fsdp"),
            P("section", "fsdp", None),
            P("section", "fsdp", None),
            P("section", "fsdp", None),
            P("section", "fsdp"),
            P("section", "fsdp", None),
            P("section", "fsdp", None),
        ),
        out_specs=(
            P("section", ("fsdp", "replica"), None),
            P("section", ("fsdp", "replica"), None),
            P("section", "fsdp"),
            P("section", "fsdp", None),
            P("section", "fsdp", None),
            P("section", "fsdp", None),
            P("section", "fsdp"),
            P("section", "fsdp", None),
            P("section", "fsdp", None),
        ),
        check_vma=False,
    )
```
